256 devices in a mesh: slab: 16 (over x, y_hi, core), chan: 16 (over y_lo, z).
Axes of the slice: x: 4, y: 4 (y_hi: 2, y_lo: 2; y = y_hi * 2 + y_lo), z: 8, core: 2. Of those that a mesh axis runs over, the one named last changes fastest.
Arguments:
- density: bfloat16 [256, 32, 16, 128], P('chan', 'slab'), may hold values from -6 to 6
- kernel_one: bfloat16 [256, 3, 3, 3, 256], P('chan'), may hold values from -0.078125 to 0.078125
- bias_one: float32 [256], P('chan'), may hold values from -3 to 3
- kernel_two: bfloat16 [256, 3, 3, 3, 256], P('chan'), may hold values from -0.078125 to 0.078125
- bias_two: float32 [256], P('chan'), may hold values from -3 to 3
Outputs:
- features: float32 [256, 32, 16, 128], P('chan', 'slab')
The draws below stay inside these ranges and needn't reach their ends.
All inputs are finite; a program needn't handle non-finite values.
Results may differ from the reference program's by a relative error of at most 0.0026.
Values may be sent and summed in bfloat16 or wider, within the bound.
No kernel may reach another device: no remote copies, remote signals or barrier semaphores. Data moves between devices by JAX's collectives and lax.ppermute only.
A program may use at most 128 MiB of HBM per device.

```python
import jax
import jax.numpy as jnp
from jax import lax

C = 256
Y = 16
X = 128
NZ = 32


def shard_levels(own_key, shape, split, least, largest):
    def one(dim, parts):
        heights = jax.random.uniform(jax.random.fold_in(jax.random.fold_in(own_key, 6), dim), (parts,), jnp.float32, least / len(split), largest / len(split))
        return jnp.repeat(jnp.exp(heights), shape[dim] // parts).reshape((-1,) + (1,) * (len(shape) - dim - 1))

    factor_of = one(*split[0])
    for cut in split[1:]:
        factor_of = factor_of * one(*cut)
    return factor_of


def normal_values(own_key, dims, spread, reach, shards=(), kind=jnp.bfloat16):
    values = spread * jax.random.normal(own_key, dims, jnp.float32)
    if shards:
        values = values * shard_levels(own_key, dims, shards, -0.22, 0.18)
    return jnp.clip(values, -reach, reach).astype(kind)


def setup_inputs(seed: int = 0) -> dict:
    splits = jax.random.split(jax.random.key(seed), 6)
    return {
        "density": normal_values(splits[0], (C, NZ, Y, X), 1.0, 6.0, ((0, 16), (1, 16))),
        "kernel_one": normal_values(splits[1], (C, 3, 3, 3, C), (27 * C) ** -0.5, 0.078125, ((0, 16),)),
        "bias_one": normal_values(splits[2], (C,), 0.5, 3.0, ((0, 16),), jnp.float32),
        "kernel_two": normal_values(splits[3], (C, 3, 3, 3, C), (27 * C) ** -0.5, 0.078125, ((0, 16),)),
        "bias_two": normal_values(splits[4], (C,), 0.5, 3.0, ((0, 16),), jnp.float32),
    }


def convolve(volume, kernel):
    padded = jnp.pad(volume, ((0, 0), (1, 1), (1, 1), (1, 1)), mode="wrap")
    result = lax.conv_general_dilated(padded[None], kernel, (1, 1, 1), "VALID", dimension_numbers=("NCDHW", "ODHWI", "NCDHW"), preferred_element_type=jnp.float32)
    return result[0]


def reference(density, kernel_one, bias_one, kernel_two, bias_two):
    first = convolve(density, kernel_one) + bias_one[:, None, None, None]
    hidden = jnp.where(first >= 0.0, first, 0.3 * first).astype(jnp.bfloat16)
    return convolve(hidden, kernel_two) + bias_two[:, None, None, None]
```

```python
import functools

import jax
import jax.numpy as jnp
from jax import lax
from jax.experimental import pallas as pl
from jax.experimental.pallas import tpu as pltpu
from jax.sharding import PartitionSpec as P

BF = jnp.bfloat16
F32 = jnp.float32
PATCH = [[2 * p, 2 * p + 1, 2 * p + 8, 2 * p + 9] for p in range(4)]
STRIDE = [[8 * y + z + 2 * p for p in range(4)] for y in range(2) for z in range(2)]
VMEM = 56 * 1024 * 1024


def call(kernel, out_shape, scratch=(), name=None):
    return pl.pallas_call(
        kernel,
        out_shape=out_shape,
        scratch_shapes=list(scratch),
        compiler_params=pltpu.CompilerParams(vmem_limit_bytes=VMEM),
        name=name,
    )


def weights_kernel(one_ref, two_ref, out_ref):
    row = lax.broadcasted_iota(jnp.int32, (256, 256), 0)
    col = lax.broadcasted_iota(jnp.int32, (256, 256), 1)
    y, p, z, c = row // 128, (row // 32) % 4, (row // 16) % 2, row % 16
    move = jnp.where(col == (2 * y + z) * 64 + p * 16 + c, 1.0, 0.0).astype(BF)
    for k, ref in enumerate((one_ref, two_ref)):
        for a in range(3):
            for b in range(3):
                for e in range(3):
                    taps = jnp.dot(ref[a, b, e], move, preferred_element_type=F32).astype(BF)
                    at = (3 * a + e) * 64
                    for i in range(4):
                        out_ref[i, k, b, :, at : at + 64] = taps[:, i * 64 : i * 64 + 64]


def conv_kernel(which, low_ref, main_ref, high_ref, w_ref, out_ref, cols, rows):
    planes = [low_ref.at[:, 0], main_ref.at[:, 0], main_ref.at[:, 1], high_ref.at[:, 0]]
    for p, ref in enumerate(planes):
        for y in range(16):
            tile = ref[:, y].reshape(64, 128)
            wide = tile.astype(F32)
            at = slice(y * 128, y * 128 + 128)
            cols[p * 192 : p * 192 + 64, at] = pltpu.roll(wide, 1, 1).astype(BF)
            cols[p * 192 + 64 : p * 192 + 128, at] = tile
            cols[p * 192 + 128 : p * 192 + 192, at] = pltpu.roll(wide, 127, 1).astype(BF)
    w = w_ref[:, which].reshape(192, 576)
    for o in range(2):
        rows[...] = jnp.dot(w, cols[o * 192 : o * 192 + 576, :], preferred_element_type=F32)
        for i in range(4):
            for y in range(16):
                total = None
                for b in range(3):
                    at = ((y + b - 1) % 16) * 128
                    part = rows[i * 48 + b * 16 : i * 48 + b * 16 + 16, at : at + 128]
                    total = part if total is None else total + part
                out_ref[i, o, y] = total.astype(out_ref.dtype)


def hidden_kernel(parts_ref, bias_ref, out_ref):
    bias = bias_ref[...]
    for o in range(2):
        total = parts_ref[0, o] + parts_ref[1, o] + parts_ref[2, o] + parts_ref[3, o] + bias
        out_ref[o] = jnp.where(total >= 0.0, total, 0.3 * total).astype(BF)


def features_kernel(parts_ref, bias_ref, out_ref, scratch):
    bias = bias_ref[...]
    for o in range(2):
        total = bias
        for s in range(4):
            total = total + parts_ref[s, o].astype(F32)
        scratch[...] = total
        for c in range(16):
            out_ref[c, o] = scratch[:, c, :]


def exchange(blocks):
    return lax.all_to_all(blocks, "chan", 0, 0, tiled=True, axis_index_groups=PATCH)


def gather(block):
    return lax.all_gather(block, "chan", axis=0, axis_index_groups=STRIDE)


def halo(main):
    head, tail = main[:, :1], main[:, 1:]
    low = lax.ppermute(tail, "slab", [(i, (i + 1) % 16) for i in range(16)])
    high = lax.ppermute(head, "slab", [((i + 1) % 16, i) for i in range(16)])
    return low, high


def convolve(which, own, w, dtype):
    main = gather(own)
    low, high = halo(main)
    return call(
        functools.partial(conv_kernel, which),
        jax.ShapeDtypeStruct((4, 2, 16, 16, 128), dtype),
        [pltpu.VMEM((768, 2048), BF), pltpu.VMEM((192, 2048), F32)],
        name="conv",
    )(low, main, high, w)


def body(density, kernel_one, bias_one, kernel_two, bias_two):
    own = jnp.transpose(density, (1, 2, 0, 3))
    w = call(weights_kernel, jax.ShapeDtypeStruct((4, 2, 3, 16, 576), BF), name="weights")(
        jnp.transpose(kernel_one, (1, 2, 3, 0, 4)), jnp.transpose(kernel_two, (1, 2, 3, 0, 4))
    )
    w = exchange(w)
    parts = exchange(convolve(0, own, w, F32))
    wide = lambda bias: jnp.broadcast_to(bias[:, None], (16, 128))
    hidden = call(hidden_kernel, jax.ShapeDtypeStruct((2, 16, 16, 128), BF), name="hidden")(
        parts, wide(bias_one)
    )
    parts = exchange(convolve(1, hidden, w, BF))
    return call(
        features_kernel,
        jax.ShapeDtypeStruct((16, 2, 16, 128), F32),
        [pltpu.VMEM((16, 16, 128), F32)],
        name="features",
    )(parts, wide(bias_two))


def solution(mesh):
    return jax.shard_map(
        body,
        mesh=mesh,
        in_specs=(
            P("chan", "slab", None, None),
            P("chan", None, None, None, None),
            P("chan"),
            P("chan", None, None, None, None),
            P("chan"),
        ),
        out_specs=P("chan", "slab", None, None),
        check_vma=False,
    )
```

```python
import functools

import jax
import jax.numpy as jnp
from jax import lax
from jax.experimental import pallas as pl
from jax.experimental.pallas import tpu as pltpu
from jax.sharding import PartitionSpec as P

BF = jnp.bfloat16
F32 = jnp.float32
PATCH = [[2 * p, 2 * p + 1, 2 * p + 8, 2 * p + 9] for p in range(4)]
STRIDE = [[8 * y + z + 2 * p for p in range(4)] for y in range(2) for z in range(2)]
VMEM = 20 * 1024 * 1024


def call(kernel, out_shape, scratch=(), name=None):
    return pl.pallas_call(
        kernel,
        out_shape=out_shape,
        scratch_shapes=list(scratch),
        compiler_params=pltpu.CompilerParams(vmem_limit_bytes=VMEM),
        name=name,
    )


def weights_kernel(one_ref, two_ref, out_ref):
    row = lax.broadcasted_iota(jnp.int32, (256, 256), 0)
    col = lax.broadcasted_iota(jnp.int32, (256, 256), 1)
    y, p, z, c = row // 128, (row // 32) % 4, (row // 16) % 2, row % 16
    move = jnp.where(col == (2 * y + z) * 64 + p * 16 + c, 1.0, 0.0).astype(BF)
    for k, ref in enumerate((one_ref, two_ref)):
        moved = jnp.dot(ref[...].reshape(432, 256), move, preferred_element_type=F32).astype(BF)
        for a in range(3):
            for b in range(3):
                for e in range(3):
                    tap = (9 * a + 3 * b + e) * 16
                    at = (3 * a + e) * 64
                    for i in range(4):
                        out_ref[i, k, b, :, at : at + 64] = moved[tap : tap + 16, i * 64 : i * 64 + 64]


def lay(ref, cols, first):
    for y in range(16):
        tile = ref[:, y].reshape(64, 128)
        at = slice(y * 128, y * 128 + 128)
        cols[first : first + 64, at] = pltpu.roll(tile, 1, 1)
        cols[first + 64 : first + 128, at] = tile
        cols[first + 128 : first + 192, at] = pltpu.roll(tile, 127, 1)


def fold(rows, i, y):
    total = None
    for b in range(3):
        at = ((y + b - 1) % 16) * 128
        part = rows[i * 48 + b * 16 : i * 48 + b * 16 + 16, at : at + 128]
        total = part if total is None else total + part
    return total


def own_kernel(which, main_ref, w_ref, out_ref, cols, rows):
    lay(main_ref.at[:, 0], cols, 0)
    lay(main_ref.at[:, 1], cols, 192)
    w = w_ref[:, which].reshape(192, 576)
    for o in range(2):
        part = w[:, 192 - o * 192 : 576 - o * 192]
        rows[...] = jnp.dot(part, cols[...], preferred_element_type=F32)
        for i in range(4):
            for y in range(16):
                out_ref[i, o, y] = fold(rows, i, y)


def halo_kernel(which, low_ref, high_ref, w_ref, own_ref, out_ref, cols, rows):
    w = w_ref[:, which].reshape(192, 576)
    for o, ref in enumerate((low_ref, high_ref)):
        lay(ref.at[:, 0], cols, 0)
        part = w[:, o * 384 : o * 384 + 192]
        rows[...] = jnp.dot(part, cols[...], preferred_element_type=F32)
        for i in range(4):
            for y in range(16):
                out_ref[i, o, y] = (own_ref[i, o, y] + fold(rows, i, y)).astype(out_ref.dtype)


def upright(bias_ref):
    row = lax.broadcasted_iota(jnp.int32, (16, 16), 0)
    col = lax.broadcasted_iota(jnp.int32, (16, 16), 1)
    return jnp.sum(jnp.where(row == col, bias_ref[...], 0.0), axis=1, keepdims=True)


def hidden_kernel(parts_ref, bias_ref, out_ref):
    bias = upright(bias_ref)
    for o in range(2):
        total = parts_ref[0, o] + parts_ref[1, o] + parts_ref[2, o] + parts_ref[3, o] + bias
        out_ref[o] = jnp.where(total >= 0.0, total, 0.3 * total).astype(BF)


def features_kernel(parts_ref, bias_ref, out_ref):
    bias = upright(bias_ref)
    for o in range(2):
        total = bias
        for s in range(4):
            total = total + parts_ref[s, o].astype(F32)
        out_ref[:, o] = jnp.swapaxes(total, 0, 1)


def exchange(blocks):
    return lax.all_to_all(blocks, "chan", 0, 0, tiled=True, axis_index_groups=PATCH)


def gather(block):
    return lax.all_gather(block, "chan", axis=0, axis_index_groups=STRIDE)


def halo(main):
    head, tail = main[:, :1], main[:, 1:]
    low = lax.ppermute(tail, "slab", [(i, (i + 1) % 16) for i in range(16)])
    high = lax.ppermute(head, "slab", [((i + 1) % 16, i) for i in range(16)])
    return low, high


def convolve(which, main, low, high, w, dtype):
    shape = (4, 2, 16, 16, 128)
    own = call(
        functools.partial(own_kernel, which),
        jax.ShapeDtypeStruct(shape, F32),
        [pltpu.VMEM((384, 2048), BF), pltpu.VMEM((192, 2048), F32)],
        name="own",
    )(main, w)
    return call(
        functools.partial(halo_kernel, which),
        jax.ShapeDtypeStruct(shape, dtype),
        [pltpu.VMEM((192, 2048), BF), pltpu.VMEM((192, 2048), F32)],
        name="halo",
    )(low, high, w, own)


def body(density, kernel_one, bias_one, kernel_two, bias_two):
    main = gather(jnp.transpose(density, (1, 2, 0, 3)))
    w = call(weights_kernel, jax.ShapeDtypeStruct((4, 2, 3, 16, 576), BF), name="weights")(
        jnp.transpose(kernel_one, (1, 2, 3, 0, 4)), jnp.transpose(kernel_two, (1, 2, 3, 0, 4))
    )
    w, main = lax.optimization_barrier((w, main))
    w = exchange(w)
    parts = exchange(convolve(0, main, *halo(main), w, F32))
    hidden = call(hidden_kernel, jax.ShapeDtypeStruct((2, 16, 16, 128), BF), name="hidden")(
        parts, bias_one[None]
    )
    main = gather(hidden)
    parts = exchange(convolve(1, main, *halo(main), w, BF))
    return call(features_kernel, jax.ShapeDtypeStruct((16, 2, 16, 128), F32), name="features")(
        parts, bias_two[None]
    )


def solution(mesh):
    return jax.shard_map(
        body,
        mesh=mesh,
        in_specs=(
            P("chan", "slab", None, None),
            P("chan", None, None, None, None),
            P("chan"),
            P("chan", None, None, None, None),
            P("chan"),
        ),
        out_specs=P("chan", "slab", None, None),
        check_vma=False,
    )
```

```python
import functools

import jax
import jax.numpy as jnp
from jax import lax
from jax.experimental import pallas as pl
from jax.experimental.pallas import tpu as pltpu
from jax.sharding import PartitionSpec as P

BF = jnp.bfloat16
F32 = jnp.float32
STRIDE = [[8 * y + z + 2 * p for p in range(4)] for y in range(2) for z in range(2)]
MATE = (0, 1, 8, 9)
CHIP = [(i, i ^ 1) for i in range(16)]
SWAP = [(i, (i + 1) % 16 if i % 2 else (i - 1) % 16) for i in range(16)]
PLANE = (16, 16, 128)
VMEM = 20 * 1024 * 1024


def call(kernel, out_shape, scratch=(), name=None, limit=VMEM, **specs):
    return pl.pallas_call(
        kernel,
        out_shape=out_shape,
        **specs,
        scratch_shapes=list(scratch),
        compiler_params=pltpu.CompilerParams(vmem_limit_bytes=limit),
        name=name,
    )


def first_kernel(density_hbm, one_hbm, two_hbm, bias_one_hbm, bias_two_hbm, *refs):
    outer_ref, inner_ref, *out, density, one, two, bias_one, bias_two, sems = refs
    pairs = (
        (density_hbm, density),
        (one_hbm, one),
        (two_hbm, two),
        (bias_one_hbm, bias_one),
        (bias_two_hbm, bias_two),
    )
    copies = [pltpu.make_async_copy(x, y, sems.at[i]) for i, (x, y) in enumerate(pairs)]
    for copy in copies:
        copy.start()
    core = lax.axis_index("slab") % 2
    me = lax.axis_index("chan")
    place = 2 * (me // 8) + me % 2
    row = lax.broadcasted_iota(jnp.int32, (256, 256), 0)
    col = lax.broadcasted_iota(jnp.int32, (256, 256), 1)
    y, p, z, c = row // 128, (row // 32) % 4, (row // 16) % 2, row % 16
    move = jnp.where(col == ((2 * y + z) ^ place) * 64 + p * 16 + c, 1.0, 0.0).astype(BF)
    copies[0].wait()
    outer_ref[...] = jnp.swapaxes(density[:, core], 0, 1)
    inner_ref[...] = jnp.swapaxes(density[:, 1 - core], 0, 1)
    for k, ref in enumerate((one, two)):
        copies[1 + k].wait()
        for a in range(3):
            taps = ref[a + core * (2 - 2 * a)].reshape(144, 256)
            moved = jnp.dot(taps, move, preferred_element_type=F32).astype(BF)
            for b in range(3):
                for e in range(3):
                    tap = (3 * b + e) * 16
                    at = (3 * a + e) * 64
                    for d in range(4):
                        out[d][k, b, :, at : at + 64] = moved[tap : tap + 16, d * 64 : d * 64 + 64]
    row = lax.broadcasted_iota(jnp.int32, (16, 16), 0)
    col = lax.broadcasted_iota(jnp.int32, (16, 16), 1)
    for k, ref in enumerate((bias_one, bias_two)):
        copies[3 + k].wait()
        bias = jnp.sum(jnp.where(row == col, ref[...], 0.0), axis=1, keepdims=True)
        out[4 + k][...] = jnp.broadcast_to(bias, (16, 128))


def conv_kernel(which, first, count, base, main_ref, *refs):
    if base:
        refs = refs[:5] + refs[9:]
    *beside_ref, w0, w1, w2, w3, r0, r1, r2, r3, cols, rows = refs
    planes = [main_ref.at[:, 2], main_ref.at[:, 0], main_ref.at[:, 1], *beside_ref]
    for a, ref in enumerate(planes[first : first + count + 2]):
        for y in range(16):
            tile = ref[:, y].reshape(64, 128)
            at = slice(y * 128, y * 128 + 128)
            cols[a * 192 : a * 192 + 64, at] = pltpu.roll(tile, 1, 1)
            cols[a * 192 + 64 : a * 192 + 128, at] = tile
            cols[a * 192 + 128 : a * 192 + 192, at] = pltpu.roll(tile, 127, 1)
    w = jnp.concatenate([w[which].reshape(48, 576) for w in (w0, w1, w2, w3)], axis=0)
    for o in range(count):
        rows[...] = jnp.dot(w, cols[o * 192 : o * 192 + 576, :], preferred_element_type=F32)
        for d, out in enumerate((r0, r1, r2, r3)):
            for y in range(16):
                total = None
                for b in range(3):
                    at = ((y + b - 1) % 16) * 128
                    part = rows[d * 48 + b * 16 : d * 48 + b * 16 + 16, at : at + 128]
                    total = part if total is None else total + part
                out[base + o, y] = total.astype(out.dtype)


def join_kernel(outer_ref, inner_ref, beyond_ref, out_ref):
    out_ref[0] = outer_ref[...]
    out_ref[1] = inner_ref[...]
    out_ref[2] = beyond_ref[...]


def leaky(parts, bias_ref):
    total = bias_ref[...]
    for part in parts:
        total = total + part[0].astype(F32)
    return jnp.where(total >= 0.0, total, 0.3 * total).astype(BF)


def outer_kernel(p0, p1, p2, p3, bias_ref, out_ref):
    out_ref[...] = leaky((p0, p1, p2, p3), bias_ref)


def inner_kernel(p0, p1, p2, p3, bias_ref, outer_ref, beyond_ref, out_ref):
    out_ref[0] = outer_ref[...]
    out_ref[1] = leaky((p0, p1, p2, p3), bias_ref)
    out_ref[2] = beyond_ref[...]


def features_kernel(p0, p1, p2, p3, bias_ref, out_ref):
    core = lax.axis_index("slab") % 2
    for o in range(2):
        total = p0[o] + bias_ref[...]
        for part in (p1, p2, p3):
            total = total + part[o].astype(F32)
        out_ref[:, core + o * (1 - 2 * core)] = jnp.swapaxes(total, 0, 1)


def exchange(blocks):
    return [blocks[0]] + [
        lax.ppermute(blocks[d], "chan", [(i, i ^ MATE[d]) for i in range(16)]) for d in (1, 2, 3)
    ]


def gather(planes):
    return lax.all_gather(planes, "chan", axis=0, axis_index_groups=STRIDE)


def swap(outer):
    return lax.ppermute(outer, "slab", SWAP)


def convolve(which, first, planes, base, dtype, *operands, **more):
    return call(
        functools.partial(conv_kernel, which, first, 1, base),
        [jax.ShapeDtypeStruct((planes,) + PLANE, t) for t in (F32, dtype, dtype, BF)],
        [pltpu.VMEM((576, 2048), BF), pltpu.VMEM((192, 2048), F32)],
        name="conv",
        **more,
    )(*operands)


def body(density, kernel_one, bias_one, kernel_two, bias_two):
    plane = jax.ShapeDtypeStruct(PLANE, BF)
    taps = pltpu.VMEM((3, 3, 3, 16, 256), BF)
    row = pltpu.VMEM((1, 16), F32)
    outer, inner, *w, bias_one, bias_two = call(
        first_kernel,
        [pltpu.VMEM(PLANE, BF)] * 2
        + [pltpu.VMEM((2, 3, 16, 576), BF)] * 4
        + [pltpu.VMEM((16, 128), F32)] * 2,
        [pltpu.VMEM((16, 2, 16, 128), BF), taps, taps, row, row, pltpu.SemaphoreType.DMA((5,))],
        name="first",
        in_specs=[pl.BlockSpec(memory_space=pltpu.HBM)] * 5,
    )(
        *(
            pltpu.with_memory_space_constraint(x, pltpu.HBM)
            for x in (
                density,
                jnp.transpose(kernel_one, (1, 2, 3, 0, 4)),
                jnp.transpose(kernel_two, (1, 2, 3, 0, 4)),
                bias_one[None],
                bias_two[None],
            )
        )
    )
    beyond = swap(outer)
    w = exchange(w)
    joined = jax.ShapeDtypeStruct((3,) + PLANE, BF)
    main = gather(call(join_kernel, joined, name="join")(outer, inner, beyond))
    w[1:], main = lax.optimization_barrier((w[1:], main))
    beside = lax.ppermute(main[:, 1], "slab", CHIP)
    parts_outer = exchange(convolve(0, 0, 1, 0, F32, main, *w))
    parts_inner = exchange(convolve(0, 1, 1, 0, F32, main, beside, *w))
    outer = call(outer_kernel, plane, name="outer")(*parts_outer, bias_one)
    beyond = swap(outer)
    main = gather(call(inner_kernel, joined, name="inner")(*parts_inner, bias_one, outer, beyond))
    beside = lax.ppermute(main[:, 1], "slab", CHIP)
    parts = convolve(1, 0, 2, 0, BF, main, *w)
    same = {6 + d: d for d in range(4)}
    parts = exchange(convolve(1, 1, 2, 1, BF, main, beside, *w, *parts, input_output_aliases=same))
    return call(features_kernel, jax.ShapeDtypeStruct((16, 2, 16, 128), F32), name="features")(
        *parts, bias_two
    )


def solution(mesh):
    return jax.shard_map(
        body,
        mesh=mesh,
        in_specs=(
            P("chan", "slab", None, None),
            P("chan", None, None, None, None),
            P("chan"),
            P("chan", None, None, None, None),
            P("chan"),
        ),
        out_specs=P("chan", "slab", None, None),
        check_vma=False,
    )
```

```python
import functools

import jax
import jax.numpy as jnp
from jax import lax
from jax.experimental import pallas as pl
from jax.experimental.pallas import tpu as pltpu
from jax.sharding import PartitionSpec as P

BF = jnp.bfloat16
F32 = jnp.float32
STRIDE = [[8 * y + z + 2 * p for p in range(4)] for y in range(2) for z in range(2)]
MATE = (0, 1, 8, 9)
CHIP = [(i, i ^ 1) for i in range(16)]
SWAP = [(i, (i + 1) % 16 if i % 2 else (i - 1) % 16) for i in range(16)]
PLANE = (16, 16, 128)
VMEM = 20 * 1024 * 1024


def call(kernel, out_shape, scratch=(), name=None, limit=VMEM, **specs):
    return pl.pallas_call(
        kernel,
        out_shape=out_shape,
        **specs,
        scratch_shapes=list(scratch),
        compiler_params=pltpu.CompilerParams(vmem_limit_bytes=limit),
        name=name,
    )


def first_kernel(density_hbm, one_hbm, two_hbm, bias_one_hbm, bias_two_hbm, *refs):
    outer_ref, inner_ref, *out, density, one, two, bias_one, bias_two, sems = refs
    pairs = (
        (density_hbm, density),
        (one_hbm, one),
        (two_hbm, two),
        (bias_one_hbm, bias_one),
        (bias_two_hbm, bias_two),
    )
    copies = [pltpu.make_async_copy(x, y, sems.at[i]) for i, (x, y) in enumerate(pairs)]
    for copy in copies:
        copy.start()
    core = lax.axis_index("slab") % 2
    me = lax.axis_index("chan")
    place = 2 * (me // 8) + me % 2
    row = lax.broadcasted_iota(jnp.int32, (256, 256), 0)
    col = lax.broadcasted_iota(jnp.int32, (256, 256), 1)
    y, p, z, c = row // 128, (row // 32) % 4, (row // 16) % 2, row % 16
    move = jnp.where(col == ((2 * y + z) ^ place) * 64 + p * 16 + c, 1.0, 0.0).astype(BF)
    copies[0].wait()
    outer_ref[...] = jnp.swapaxes(density[:, core], 0, 1)
    inner_ref[...] = jnp.swapaxes(density[:, 1 - core], 0, 1)
    for k, ref in enumerate((one, two)):
        copies[1 + k].wait()
        for a in range(3):
            taps = ref[a + core * (2 - 2 * a)].reshape(144, 256)
            moved = jnp.dot(taps, move, preferred_element_type=F32).astype(BF)
            for b in range(3):
                for e in range(3):
                    tap = (3 * b + e) * 16
                    at = (3 * a + e) * 64
                    for d in range(4):
                        out[d][k, b, :, at : at + 64] = moved[tap : tap + 16, d * 64 : d * 64 + 64]
    row = lax.broadcasted_iota(jnp.int32, (16, 16), 0)
    col = lax.broadcasted_iota(jnp.int32, (16, 16), 1)
    for k, ref in enumerate((bias_one, bias_two)):
        copies[3 + k].wait()
        bias = jnp.sum(jnp.where(row == col, ref[...], 0.0), axis=1, keepdims=True)
        out[4 + k][...] = jnp.broadcast_to(bias, (16, 128))


def conv_kernel(which, first, count, base, main_ref, *refs):
    if base:
        refs = refs[:5] + refs[9:]
    *beside_ref, w0, w1, w2, w3, r0, r1, r2, r3, cols, rows = refs
    planes = [main_ref.at[:, 2], main_ref.at[:, 0], main_ref.at[:, 1], *beside_ref]
    for a, ref in enumerate(planes[first : first + count + 2]):
        for y in range(16):
            tile = ref[:, y].reshape(64, 128)
            at = slice(y * 128, y * 128 + 128)
            cols[a * 192 : a * 192 + 64, at] = pltpu.roll(tile, 1, 1)
            cols[a * 192 + 64 : a * 192 + 128, at] = tile
            cols[a * 192 + 128 : a * 192 + 192, at] = pltpu.roll(tile, 127, 1)
    w = jnp.concatenate([w[which].reshape(48, 576) for w in (w0, w1, w2, w3)], axis=0)
    for o in range(count):
        rows[...] = jnp.dot(w, cols[o * 192 : o * 192 + 576, :], preferred_element_type=F32)
        for d, out in enumerate((r0, r1, r2, r3)):
            for y in range(16):
                total = None
                for b in range(3):
                    at = ((y + b - 1) % 16) * 128
                    part = rows[d * 48 + b * 16 : d * 48 + b * 16 + 16, at : at + 128]
                    total = part if total is None else total + part
                out[base + o, y] = total.astype(out.dtype)


def join_kernel(outer_ref, inner_ref, beyond_ref, out_ref):
    out_ref[0] = outer_ref[...]
    out_ref[1] = inner_ref[...]
    out_ref[2] = beyond_ref[...]


def leaky(parts, bias_ref):
    total = bias_ref[...]
    for part in parts:
        total = total + part[0].astype(F32)
    return jnp.where(total >= 0.0, total, 0.3 * total).astype(BF)


def outer_kernel(p0, p1, p2, p3, bias_ref, out_ref):
    out_ref[...] = leaky((p0, p1, p2, p3), bias_ref)


def inner_kernel(p0, p1, p2, p3, bias_ref, outer_ref, beyond_ref, out_ref):
    out_ref[0] = outer_ref[...]
    out_ref[1] = leaky((p0, p1, p2, p3), bias_ref)
    out_ref[2] = beyond_ref[...]


def features_kernel(p0, p1, p2, p3, bias_ref, out_ref):
    core = lax.axis_index("slab") % 2
    for o in range(2):
        total = p0[o] + bias_ref[...]
        for part in (p1, p2, p3):
            total = total + part[o].astype(F32)
        out_ref[:, core + o * (1 - 2 * core)] = jnp.swapaxes(total, 0, 1)


def exchange(blocks):
    return [blocks[0]] + [
        lax.ppermute(blocks[d], "chan", [(i, i ^ MATE[d]) for i in range(16)]) for d in (1, 2, 3)
    ]


def gather(planes):
    return lax.all_gather(planes, "chan", axis=0, axis_index_groups=STRIDE)


def swap(outer):
    return lax.ppermute(outer, "slab", SWAP)


def convolve(which, first, planes, base, dtype, *operands, **more):
    return call(
        functools.partial(conv_kernel, which, first, 1, base),
        [jax.ShapeDtypeStruct((planes,) + PLANE, t) for t in (F32, dtype, dtype, dtype)],
        [pltpu.VMEM((576, 2048), BF), pltpu.VMEM((192, 2048), F32)],
        name="conv",
        **more,
    )(*operands)


def body(density, kernel_one, bias_one, kernel_two, bias_two):
    plane = jax.ShapeDtypeStruct(PLANE, BF)
    taps = pltpu.VMEM((3, 3, 3, 16, 256), BF)
    row = pltpu.VMEM((1, 16), F32)
    outer, inner, *w, bias_one, bias_two = call(
        first_kernel,
        [pltpu.VMEM(PLANE, BF)] * 2
        + [pltpu.VMEM((2, 3, 16, 576), BF)] * 4
        + [pltpu.VMEM((16, 128), F32)] * 2,
        [pltpu.VMEM((16, 2, 16, 128), BF), taps, taps, row, row, pltpu.SemaphoreType.DMA((5,))],
        name="first",
        in_specs=[pl.BlockSpec(memory_space=pltpu.HBM)] * 5,
    )(
        *(
            pltpu.with_memory_space_constraint(x, pltpu.HBM)
            for x in (
                density,
                jnp.transpose(kernel_one, (1, 2, 3, 0, 4)),
                jnp.transpose(kernel_two, (1, 2, 3, 0, 4)),
                bias_one[None],
                bias_two[None],
            )
        )
    )
    beyond = swap(outer)
    w = exchange(w)
    joined = jax.ShapeDtypeStruct((3,) + PLANE, BF)
    main = gather(call(join_kernel, joined, name="join")(outer, inner, beyond))
    w[1:], main = lax.optimization_barrier((w[1:], main))
    beside = lax.ppermute(main[:, 1], "slab", CHIP)
    parts_outer = exchange(convolve(0, 0, 1, 0, BF, main, *w))
    parts_inner = exchange(convolve(0, 1, 1, 0, F32, main, beside, *w))
    outer = call(outer_kernel, plane, name="outer")(*parts_outer, bias_one)
    beyond = swap(outer)
    main = gather(call(inner_kernel, joined, name="inner")(*parts_inner, bias_one, outer, beyond))
    beside = lax.ppermute(main[:, 1], "slab", CHIP)
    parts = convolve(1, 0, 2, 0, BF, main, *w)
    same = {6 + d: d for d in range(4)}
    parts = exchange(convolve(1, 1, 2, 1, BF, main, beside, *w, *parts, input_output_aliases=same))
    return call(features_kernel, jax.ShapeDtypeStruct((16, 2, 16, 128), F32), name="features")(
        *parts, bias_two
    )


def solution(mesh):
    return jax.shard_map(
        body,
        mesh=mesh,
        in_specs=(
            P("chan", "slab", None, None),
            P("chan", None, None, None, None),
            P("chan"),
            P("chan", None, None, None, None),
            P("chan"),
        ),
        out_specs=P("chan", "slab", None, None),
        check_vma=False,
    )
```

```python
import functools

import jax
import jax.numpy as jnp
from jax import lax
from jax.experimental import pallas as pl
from jax.experimental.pallas import tpu as pltpu
from jax.sharding import PartitionSpec as P

BF = jnp.bfloat16
F32 = jnp.float32
STRIDE = [[8 * y + z + 2 * p for p in range(4)] for y in range(2) for z in range(2)]
MATE = (0, 1, 8, 9)
CHIP = [(i, i ^ 1) for i in range(16)]
SWAP = [(i, (i + 1) % 16 if i % 2 else (i - 1) % 16) for i in range(16)]
PLANE = (16, 16, 128)
VMEM = 20 * 1024 * 1024


def call(kernel, out_shape, scratch=(), name=None, limit=VMEM, **specs):
    return pl.pallas_call(
        kernel,
        out_shape=out_shape,
        **specs,
        scratch_shapes=list(scratch),
        compiler_params=pltpu.CompilerParams(vmem_limit_bytes=limit),
        name=name,
    )


def first_kernel(density_hbm, one_hbm, two_hbm, bias_one_hbm, bias_two_hbm, *refs):
    outer_ref, inner_ref, *out, density, one, two, bias_one, bias_two, sems = refs
    pairs = (
        (density_hbm, density),
        (one_hbm, one),
        (two_hbm, two),
        (bias_one_hbm, bias_one),
        (bias_two_hbm, bias_two),
    )
    copies = [pltpu.make_async_copy(x, y, sems.at[i]) for i, (x, y) in enumerate(pairs)]
    for copy in copies:
        copy.start()
    core = lax.axis_index("slab") % 2
    me = lax.axis_index("chan")
    place = 2 * (me // 8) + me % 2
    row = lax.broadcasted_iota(jnp.int32, (256, 256), 0)
    col = lax.broadcasted_iota(jnp.int32, (256, 256), 1)
    y, p, z, c = row // 128, (row // 32) % 4, (row // 16) % 2, row % 16
    move = jnp.where(col == ((2 * y + z) ^ place) * 64 + p * 16 + c, 1.0, 0.0).astype(BF)
    copies[0].wait()
    outer_ref[...] = jnp.swapaxes(density[:, core], 0, 1)
    inner_ref[...] = jnp.swapaxes(density[:, 1 - core], 0, 1)
    for k, ref in enumerate((one, two)):
        copies[1 + k].wait()
        for a in range(3):
            taps = ref[a + core * (2 - 2 * a)].reshape(144, 256)
            moved = jnp.dot(taps, move, preferred_element_type=F32).astype(BF)
            for b in range(3):
                for e in range(3):
                    tap = (3 * b + e) * 16
                    at = (3 * a + e) * 64
                    for d in range(4):
                        out[d][k, b, :, at : at + 64] = moved[tap : tap + 16, d * 64 : d * 64 + 64]
    row = lax.broadcasted_iota(jnp.int32, (16, 16), 0)
    col = lax.broadcasted_iota(jnp.int32, (16, 16), 1)
    for k, ref in enumerate((bias_one, bias_two)):
        copies[3 + k].wait()
        bias = jnp.sum(jnp.where(row == col, ref[...], 0.0), axis=1, keepdims=True)
        out[4 + k][...] = jnp.broadcast_to(bias, (16, 128))


def lay(ref, cols, a):
    for y in range(16):
        tile = ref[:, y].reshape(64, 128)
        at = slice(y * 128, y * 128 + 128)
        cols[a * 192 : a * 192 + 64, at] = pltpu.roll(tile, 1, 1)
        cols[a * 192 + 64 : a * 192 + 128, at] = tile
        cols[a * 192 + 128 : a * 192 + 192, at] = pltpu.roll(tile, 127, 1)


def matrix(which, w_refs):
    return jnp.concatenate([w[which].reshape(48, 576) for w in w_refs], axis=0)


def fold(rows, outs, plane):
    for d, out in enumerate(outs):
        for y in range(16):
            total = None
            for b in range(3):
                at = ((y + b - 1) % 16) * 128
                part = rows[d * 48 + b * 16 : d * 48 + b * 16 + 16, at : at + 128]
                total = part if total is None else total + part
            out[plane, y] = total.astype(out.dtype)


def outside_kernel(which, main_ref, w0, w1, w2, w3, r0, r1, r2, r3, part, cols, rows):
    for a, p in enumerate((2, 0, 1)):
        lay(main_ref.at[:, p], cols, a)
    w = matrix(which, (w0, w1, w2, w3))
    rows[...] = jnp.dot(w, cols[...], preferred_element_type=F32)
    fold(rows, (r0, r1, r2, r3), 0)
    part[...] = jnp.dot(w[:, :384], cols[192:576, :], preferred_element_type=F32)


def first_outside_kernel(main_ref, w0, w1, w2, w3, r0, r1, r2, r3, cols, rows):
    for a, p in enumerate((2, 0, 1)):
        lay(main_ref.at[:, p], cols, a)
    w = matrix(0, (w0, w1, w2, w3))
    rows[...] = jnp.dot(w, cols[...], preferred_element_type=F32)
    fold(rows, (r0, r1, r2, r3), 0)


def inside_kernel(which, plane, share, beside_ref, w0, w1, w2, w3, *refs):
    r0, r1, r2, r3, side, rows = refs[4 * plane :]
    lay(beside_ref, side, 0)
    w = matrix(which, (w0, w1, w2, w3))
    if which:
        most = share[...]
    else:
        most = jnp.dot(w[:, :384], share[192:576, :], preferred_element_type=F32)
    rows[...] = most + jnp.dot(w[:, 384:], side[...], preferred_element_type=F32)
    fold(rows, (r0, r1, r2, r3), plane)


def join_kernel(outer_ref, inner_ref, beyond_ref, out_ref):
    out_ref[0] = outer_ref[...]
    out_ref[1] = inner_ref[...]
    out_ref[2] = beyond_ref[...]


def leaky(parts, bias_ref):
    total = bias_ref[...]
    for part in parts:
        total = total + part[0].astype(F32)
    return jnp.where(total >= 0.0, total, 0.3 * total).astype(BF)


def outer_kernel(p0, p1, p2, p3, bias_ref, out_ref):
    out_ref[...] = leaky((p0, p1, p2, p3), bias_ref)


def inner_kernel(p0, p1, p2, p3, bias_ref, outer_ref, beyond_ref, out_ref):
    out_ref[0] = outer_ref[...]
    out_ref[1] = leaky((p0, p1, p2, p3), bias_ref)
    out_ref[2] = beyond_ref[...]


def features_kernel(p0, p1, p2, p3, bias_ref, out_ref):
    core = lax.axis_index("slab") % 2
    for o in range(2):
        total = p0[o] + bias_ref[...]
        for part in (p1, p2, p3):
            total = total + part[o].astype(F32)
        out_ref[:, core + o * (1 - 2 * core)] = jnp.swapaxes(total, 0, 1)


def exchange(blocks):
    return [blocks[0]] + [
        lax.ppermute(blocks[d], "chan", [(i, i ^ MATE[d]) for i in range(16)]) for d in (1, 2, 3)
    ]


def gather(planes):
    return lax.all_gather(planes, "chan", axis=0, axis_index_groups=STRIDE)


def swap(outer):
    return lax.ppermute(outer, "slab", SWAP)


def sums(planes, dtype):
    return [jax.ShapeDtypeStruct((planes,) + PLANE, t) for t in (F32, dtype, dtype, dtype)]


def outside(which, planes, dtype, *operands):
    cols, rows = pltpu.VMEM((576, 2048), BF), pltpu.VMEM((192, 2048), F32)
    *parts, share = call(
        functools.partial(outside_kernel, which) if which else first_outside_kernel,
        sums(planes, dtype)
        + [jax.ShapeDtypeStruct((192, 2048), F32) if which else jax.ShapeDtypeStruct((576, 2048), BF)],
        [cols, rows] if which else [rows],
        name="outside",
    )(*operands)
    return parts, share


def inside(which, planes, dtype, *operands, **more):
    return call(
        functools.partial(inside_kernel, which, planes - 1),
        sums(planes, dtype),
        [pltpu.VMEM((192, 2048), BF), pltpu.VMEM((192, 2048), F32)],
        name="inside",
        **more,
    )(*operands)


def body(density, kernel_one, bias_one, kernel_two, bias_two):
    plane = jax.ShapeDtypeStruct(PLANE, BF)
    taps = pltpu.VMEM((3, 3, 3, 16, 256), BF)
    row = pltpu.VMEM((1, 16), F32)
    outer, inner, *w, bias_one, bias_two = call(
        first_kernel,
        [pltpu.VMEM(PLANE, BF)] * 2
        + [pltpu.VMEM((2, 3, 16, 576), BF)] * 4
        + [pltpu.VMEM((16, 128), F32)] * 2,
        [pltpu.VMEM((16, 2, 16, 128), BF), taps, taps, row, row, pltpu.SemaphoreType.DMA((5,))],
        name="first",
        in_specs=[pl.BlockSpec(memory_space=pltpu.HBM)] * 5,
    )(
        *(
            pltpu.with_memory_space_constraint(x, pltpu.HBM)
            for x in (
                density,
                jnp.transpose(kernel_one, (1, 2, 3, 0, 4)),
                jnp.transpose(kernel_two, (1, 2, 3, 0, 4)),
                bias_one[None],
                bias_two[None],
            )
        )
    )
    beyond = swap(outer)
    w = exchange(w)
    joined = jax.ShapeDtypeStruct((3,) + PLANE, BF)
    main = gather(call(join_kernel, joined, name="join")(outer, inner, beyond))
    w[1:], main = lax.optimization_barrier((w[1:], main))
    beside = lax.ppermute(main[:, 1], "slab", CHIP)
    parts_outer, cols = outside(0, 1, BF, main, *w)
    parts_outer = exchange(parts_outer)
    parts_inner = exchange(inside(0, 1, F32, cols, beside, *w))
    outer = call(outer_kernel, plane, name="outer")(*parts_outer, bias_one)
    beyond = swap(outer)
    main = gather(call(inner_kernel, joined, name="inner")(*parts_inner, bias_one, outer, beyond))
    beside = lax.ppermute(main[:, 1], "slab", CHIP)
    parts, cols = outside(1, 2, BF, main, *w)
    same = {6 + d: d for d in range(4)}
    parts = exchange(inside(1, 2, BF, cols, beside, *w, *parts, input_output_aliases=same))
    return call(features_kernel, jax.ShapeDtypeStruct((16, 2, 16, 128), F32), name="features")(
        *parts, bias_two
    )


def solution(mesh):
    return jax.shard_map(
        body,
        mesh=mesh,
        in_specs=(
            P("chan", "slab", None, None),
            P("chan", None, None, None, None),
            P("chan"),
            P("chan", None, None, None, None),
            P("chan"),
        ),
        out_specs=P("chan", "slab", None, None),
        check_vma=False,
    )
```

```python
import functools

import jax
import jax.numpy as jnp
from jax import lax
from jax.experimental import pallas as pl
from jax.experimental.pallas import tpu as pltpu
from jax.sharding import PartitionSpec as P

BF = jnp.bfloat16
F32 = jnp.float32
STRIDE = [[8 * y + z + 2 * p for p in range(4)] for y in range(2) for z in range(2)]
MATE = (0, 1, 8, 9)
CHIP = [(i, i ^ 1) for i in range(16)]
SWAP = [(i, (i + 1) % 16 if i % 2 else (i - 1) % 16) for i in range(16)]
PLANE = (16, 16, 128)
VMEM = 20 * 1024 * 1024


def call(kernel, out_shape, scratch=(), name=None, limit=VMEM, **specs):
    return pl.pallas_call(
        kernel,
        out_shape=out_shape,
        **specs,
        scratch_shapes=list(scratch),
        compiler_params=pltpu.CompilerParams(vmem_limit_bytes=limit),
        name=name,
    )


def first_kernel(density_hbm, one_hbm, two_hbm, bias_one_hbm, bias_two_hbm, *refs):
    outer_ref, inner_ref, *out, density, one, two, bias_one, bias_two, sems = refs
    pairs = (
        (density_hbm, density),
        (one_hbm, one),
        (two_hbm, two),
        (bias_one_hbm, bias_one),
        (bias_two_hbm, bias_two),
    )
    copies = [pltpu.make_async_copy(x, y, sems.at[i]) for i, (x, y) in enumerate(pairs)]
    for copy in copies:
        copy.start()
    core = lax.axis_index("slab") % 2
    me = lax.axis_index("chan")
    place = 2 * (me // 8) + me % 2
    row = lax.broadcasted_iota(jnp.int32, (256, 256), 0)
    col = lax.broadcasted_iota(jnp.int32, (256, 256), 1)
    y, p, z, c = row // 128, (row // 32) % 4, (row // 16) % 2, row % 16
    move = jnp.where(col == ((2 * y + z) ^ place) * 64 + p * 16 + c, 1.0, 0.0).astype(BF)
    copies[0].wait()
    outer_ref[...] = jnp.swapaxes(density[:, core], 0, 1)
    inner_ref[...] = jnp.swapaxes(density[:, 1 - core], 0, 1)
    for k, ref in enumerate((one, two)):
        copies[1 + k].wait()
        for a in range(3):
            taps = ref[a + core * (2 - 2 * a)].reshape(144, 256)
            moved = jnp.dot(taps, move, preferred_element_type=F32).astype(BF)
            for b in range(3):
                for e in range(3):
                    tap = (3 * b + e) * 16
                    at = (3 * a + e) * 64
                    for d in range(4):
                        out[d][k, b, :, at : at + 64] = moved[tap : tap + 16, d * 64 : d * 64 + 64]
    row = lax.broadcasted_iota(jnp.int32, (16, 16), 0)
    col = lax.broadcasted_iota(jnp.int32, (16, 16), 1)
    for k, ref in enumerate((bias_one, bias_two)):
        copies[3 + k].wait()
        bias = jnp.sum(jnp.where(row == col, ref[...], 0.0), axis=1, keepdims=True)
        out[4 + k][...] = jnp.broadcast_to(bias, (16, 128))


def lay(ref, cols, a):
    for y in range(16):
        tile = ref[:, y].reshape(64, 128)
        at = slice(y * 128, y * 128 + 128)
        cols[a * 192 : a * 192 + 64, at] = pltpu.roll(tile, 1, 1)
        cols[a * 192 + 64 : a * 192 + 128, at] = tile
        cols[a * 192 + 128 : a * 192 + 192, at] = pltpu.roll(tile, 127, 1)


def matrix(which, w_refs):
    return jnp.concatenate([w[which].reshape(48, 576) for w in w_refs], axis=0)


def fold(rows, outs, plane):
    for d, out in enumerate(outs):
        for y in range(16):
            total = None
            for b in range(3):
                at = ((y + b - 1) % 16) * 128
                part = rows[d * 48 + b * 16 : d * 48 + b * 16 + 16, at : at + 128]
                total = part if total is None else total + part
            out[plane, y] = total.astype(out.dtype)


def outside_kernel(which, main_ref, w0, w1, w2, w3, r0, r1, r2, r3, part, cols, rows):
    for a, p in enumerate((2, 0, 1)):
        lay(main_ref.at[:, p], cols, a)
    w = matrix(which, (w0, w1, w2, w3))
    rows[...] = jnp.dot(w, cols[...], preferred_element_type=F32)
    fold(rows, (r0, r1, r2, r3), 0)
    part[...] = jnp.dot(w[:, :384], cols[192:576, :], preferred_element_type=F32)


def first_outside_kernel(main_ref, w0, w1, w2, w3, r0, r1, r2, r3, cols, rows):
    for a, p in enumerate((2, 0, 1)):
        lay(main_ref.at[:, p], cols, a)
    w = matrix(0, (w0, w1, w2, w3))
    rows[...] = jnp.dot(w, cols[...], preferred_element_type=F32)
    fold(rows, (r0, r1, r2, r3), 0)


def inside_kernel(which, plane, share, beside_ref, w0, w1, w2, w3, *refs):
    r0, r1, r2, r3, side, rows = refs[4 * plane :]
    lay(beside_ref, side, 0)
    w = matrix(which, (w0, w1, w2, w3))
    if which:
        most = share[...]
    else:
        most = jnp.dot(w[:, :384], share[192:576, :], preferred_element_type=F32)
    rows[...] = most + jnp.dot(w[:, 384:], side[...], preferred_element_type=F32)
    fold(rows, (r0, r1, r2, r3), plane)


def join_kernel(outer_ref, inner_ref, beyond_ref, out_ref):
    out_ref[0] = outer_ref[...]
    out_ref[1] = inner_ref[...]
    out_ref[2] = beyond_ref[...]


def leaky(parts, bias_ref):
    total = bias_ref[...]
    for part in parts:
        total = total + part[0].astype(F32)
    return jnp.where(total >= 0.0, total, 0.3 * total).astype(BF)


def outer_kernel(p0, p1, p2, p3, bias_ref, out_ref):
    out_ref[...] = leaky((p0, p1, p2, p3), bias_ref)


def inner_kernel(p0, p1, p2, p3, bias_ref, outer_ref, beyond_ref, out_ref):
    out_ref[0] = outer_ref[...]
    out_ref[1] = leaky((p0, p1, p2, p3), bias_ref)
    out_ref[2] = beyond_ref[...]


def features_kernel(p0, p1, p2, p3, bias_ref, out_ref):
    core = lax.axis_index("slab") % 2
    for o in range(2):
        total = p0[o] + bias_ref[...]
        for part in (p1, p2, p3):
            total = total + part[o].astype(F32)
        out_ref[:, core + o * (1 - 2 * core)] = jnp.swapaxes(total, 0, 1)


def exchange(blocks, order=(1, 2, 3)):
    got = {
        d: lax.ppermute(blocks[d], "chan", [(i, i ^ MATE[d]) for i in range(16)]) for d in order
    }
    return [blocks[0]] + [got[d] for d in (1, 2, 3)]


def gather(planes):
    return lax.all_gather(planes, "chan", axis=0, axis_index_groups=STRIDE)


def swap(outer):
    return lax.ppermute(outer, "slab", SWAP)


def sums(planes, dtype):
    return [jax.ShapeDtypeStruct((planes,) + PLANE, t) for t in (F32, dtype, dtype, dtype)]


def outside(which, planes, dtype, *operands):
    cols, rows = pltpu.VMEM((576, 2048), BF), pltpu.VMEM((192, 2048), F32)
    *parts, share = call(
        functools.partial(outside_kernel, which) if which else first_outside_kernel,
        sums(planes, dtype)
        + [jax.ShapeDtypeStruct((192, 2048), F32) if which else jax.ShapeDtypeStruct((576, 2048), BF)],
        [cols, rows] if which else [rows],
        name="outside",
    )(*operands)
    return parts, share


def inside(which, planes, dtype, *operands, **more):
    return call(
        functools.partial(inside_kernel, which, planes - 1),
        sums(planes, dtype),
        [pltpu.VMEM((192, 2048), BF), pltpu.VMEM((192, 2048), F32)],
        name="inside",
        **more,
    )(*operands)


def body(density, kernel_one, bias_one, kernel_two, bias_two):
    plane = jax.ShapeDtypeStruct(PLANE, BF)
    taps = pltpu.VMEM((3, 3, 3, 16, 256), BF)
    row = pltpu.VMEM((1, 16), F32)
    outer, inner, *w, bias_one, bias_two = call(
        first_kernel,
        [pltpu.VMEM(PLANE, BF)] * 2
        + [pltpu.VMEM((2, 3, 16, 576), BF)] * 4
        + [pltpu.VMEM((16, 128), F32)] * 2,
        [pltpu.VMEM((16, 2, 16, 128), BF), taps, taps, row, row, pltpu.SemaphoreType.DMA((5,))],
        name="first",
        in_specs=[pl.BlockSpec(memory_space=pltpu.HBM)] * 5,
    )(
        *(
            pltpu.with_memory_space_constraint(x, pltpu.HBM)
            for x in (
                density,
                jnp.transpose(kernel_one, (1, 2, 3, 0, 4)),
                jnp.transpose(kernel_two, (1, 2, 3, 0, 4)),
                bias_one[None],
                bias_two[None],
            )
        )
    )
    beyond = swap(outer)
    w = exchange(w, (3, 2, 1))
    joined = jax.ShapeDtypeStruct((3,) + PLANE, BF)
    main = gather(call(join_kernel, joined, name="join")(outer, inner, beyond))
    w[1:], main = lax.optimization_barrier((w[1:], main))
    beside = lax.ppermute(main[:, 1], "slab", CHIP)
    parts_outer, cols = outside(0, 1, BF, main, *w)
    parts_outer = exchange(parts_outer)
    parts_inner = exchange(inside(0, 1, F32, cols, beside, *w))
    outer = call(outer_kernel, plane, name="outer")(*parts_outer, bias_one)
    beyond = swap(outer)
    main = gather(call(inner_kernel, joined, name="inner")(*parts_inner, bias_one, outer, beyond))
    beside = lax.ppermute(main[:, 1], "slab", CHIP)
    parts, cols = outside(1, 2, BF, main, *w)
    same = {6 + d: d for d in range(4)}
    parts = exchange(inside(1, 2, BF, cols, beside, *w, *parts, input_output_aliases=same))
    return call(features_kernel, jax.ShapeDtypeStruct((16, 2, 16, 128), F32), name="features")(
        *parts, bias_two
    )


def solution(mesh):
    return jax.shard_map(
        body,
        mesh=mesh,
        in_specs=(
            P("chan", "slab", None, None),
            P("chan", None, None, None, None),
            P("chan"),
            P("chan", None, None, None, None),
            P("chan"),
        ),
        out_specs=P("chan", "slab", None, None),
        check_vma=False,
    )
```
